256 devices in a mesh: ctx: 16 (over z, core), pipe: 4 (over y), tp: 4 (over x).
Axes of the slice: x: 4, y: 4, z: 8, core: 2. Of those that a mesh axis runs over, the one named last changes fastest.
Arguments:
- hidden: bfloat16 [16, 256, 4096], P('ctx', 'tp'), may hold values from -6 to 6
- norm_gain: bfloat16 [4, 4096], P('pipe'), may hold values from 0.25 to 1.75
- w_query: bfloat16 [4, 4096, 2048], P('pipe', None, 'tp'), may hold values from -0.09375 to 0.09375
- key_weight: bfloat16 [4, 4096, 512], P('pipe', None, 'tp'), may hold values from -0.09375 to 0.09375
- value_weight: bfloat16 [4, 4096, 512], P('pipe', None, 'tp'), may hold values from -0.09375 to 0.09375
- w_out: bfloat16 [4, 2048, 4096], P('pipe', 'tp'), may hold values from -0.125 to 0.125
Outputs:
- layer_states: bfloat16 [4, 16, 256, 4096], P('pipe', 'ctx', 'tp')
The draws below stay inside these ranges and needn't reach their ends.
All inputs are finite; a program needn't handle non-finite values.
Results may differ from the reference program's by a relative error of at most 0.022.
Values may be sent and summed in bfloat16 or wider, within the bound.
No kernel may reach another device: no remote copies, remote signals or barrier semaphores. Data moves between devices by JAX's collectives and lax.ppermute only.
A program may use at most 128 MiB of HBM per device.

```python
import jax
import jax.numpy as jnp
from jax import lax

MODEL_WIDTH = 4096
HQ = 16
KEY_VALUE_HEADS = 4
HEAD_SIZE = 128
BLOCK_TOKENS = 256
CONTEXT_BLOCKS = 16
LAYER_COUNT = 4
N_TP = 4


def steps_of(stream_key, extent, shards, least, high):
    def one(dim, parts):
        heights = jax.random.uniform(jax.random.fold_in(jax.random.fold_in(stream_key, 6), dim), (parts,), jnp.float32, least / len(shards), high / len(shards))
        return jnp.repeat(jnp.exp(heights), extent[dim] // parts).reshape((-1,) + (1,) * (len(extent) - dim - 1))

    gain = one(*shards[0])
    for cut in shards[1:]:
        gain = gain * one(*cut)
    return gain


def normal_values(own_key, dims, spread, reach, split=(), kind=jnp.bfloat16):
    factor_of = steps_of(own_key, dims, split, -0.22, 0.18) if split else 1.0
    values = jax.random.normal(own_key, dims, jnp.float32) * spread * factor_of
    return jnp.minimum(jnp.maximum(values, -reach), reach).astype(kind)


def setup_inputs(seed: int = 0) -> dict:
    splits = jax.random.split(jax.random.key(seed), 7)
    return {
        "hidden": normal_values(splits[0], (CONTEXT_BLOCKS, BLOCK_TOKENS, MODEL_WIDTH), 1.0, 6.0, ((0, 16), (1, 4))),
        "norm_gain": jnp.clip(1.0 + 0.15 * jax.random.normal(splits[1], (LAYER_COUNT, MODEL_WIDTH), jnp.float32), 0.25, 1.75).astype(jnp.bfloat16),
        "w_query": normal_values(splits[2], (LAYER_COUNT, MODEL_WIDTH, HQ * HEAD_SIZE), MODEL_WIDTH ** -0.5, 0.09375, ((0, 4), (2, 4))),
        "key_weight": normal_values(splits[3], (LAYER_COUNT, MODEL_WIDTH, KEY_VALUE_HEADS * HEAD_SIZE), MODEL_WIDTH ** -0.5, 0.09375, ((0, 4), (2, 4))),
        "value_weight": normal_values(splits[4], (LAYER_COUNT, MODEL_WIDTH, KEY_VALUE_HEADS * HEAD_SIZE), MODEL_WIDTH ** -0.5, 0.09375, ((0, 4), (2, 4))),
        "w_out": normal_values(splits[5], (LAYER_COUNT, HQ * HEAD_SIZE, MODEL_WIDTH), (HQ * HEAD_SIZE) ** -0.5, 0.125, ((0, 4), (1, 4))),
    }


rope_theta = 500000.0
norm_eps = 1e-05

def rotary_embed(values, token_positions):
    head_dim = values.shape[-1]
    half_size = head_dim // 2
    frequency = rope_theta ** (-(jnp.arange(half_size, dtype=jnp.float32) * 2.0 / head_dim))
    angles = token_positions[:, :, None] * frequency[None, None, :]
    cosine = jnp.concatenate([jnp.cos(angles), jnp.cos(angles)], -1)[:, :, None, :]
    sine_part = jnp.concatenate([jnp.sin(angles), jnp.sin(angles)], -1)[:, :, None, :]
    first_half = values[..., :half_size]
    second_half = values[..., half_size:]
    rotated = jnp.concatenate([-second_half, first_half], -1)
    return values * cosine + rotated * sine_part

def attend(queries, projected_keys, projected_values, block_ids, anchor_key, anchor_value):
    block_count, block_len, head_count, head_dim = queries.shape
    kv_heads = projected_keys.shape[2]
    groups = head_count // kv_heads
    all_keys = jnp.concatenate([jnp.broadcast_to(anchor_key[None], projected_keys.shape), projected_keys], 1)
    all_values = jnp.concatenate([jnp.broadcast_to(anchor_value[None], projected_values.shape), projected_values], 1)
    grouped = queries.reshape(block_count, block_len, kv_heads, groups, head_dim)
    scores = jnp.einsum('nqkgd,nskd->nkgqs', grouped.astype(jnp.float32), all_keys.astype(jnp.float32)) / jnp.sqrt(jnp.float32(head_dim))
    query_pos = jnp.arange(block_len, dtype=jnp.int32)[:, None]
    key_pos = jnp.arange(2 * block_len, dtype=jnp.int32)[None, :]
    own_ok = (key_pos >= block_len) & (key_pos - block_len <= query_pos)
    anchor_ok = (key_pos < block_len)[None] & (block_ids > 0)[:, None, None]
    allowed = own_ok[None] | anchor_ok
    scores = jnp.where(allowed[:, None, None], scores, jnp.float32(-1e+30))
    highest = lax.optimization_barrier(jnp.max(scores, -1, keepdims=True))
    powers = jnp.exp(scores - highest)
    weights = (powers / lax.optimization_barrier(jnp.sum(powers, -1, keepdims=True))).astype(jnp.bfloat16)
    mixed = jnp.einsum('nkgqs,nskd->nqkgd', weights.astype(jnp.float32), all_values.astype(jnp.float32))
    return mixed.astype(jnp.bfloat16).reshape(block_count, block_len, head_count * head_dim)

def reference(hidden, norm_gain, w_query, key_weight, value_weight, w_out):
    state = hidden
    layer_outputs = []
    block_ids = jnp.arange(CONTEXT_BLOCKS, dtype=jnp.int32)
    token_positions = (block_ids[:, None] * BLOCK_TOKENS + jnp.arange(BLOCK_TOKENS, dtype=jnp.int32)[None, :]).astype(jnp.float32)
    share = HQ * HEAD_SIZE // N_TP
    for current_layer in range(LAYER_COUNT):
        values32 = state.astype(jnp.float32)
        scale_rows = lax.rsqrt(lax.optimization_barrier(jnp.mean(values32 * values32, -1, keepdims=True)) + norm_eps)
        normed = (values32 * scale_rows * norm_gain[current_layer].astype(jnp.float32)).astype(jnp.bfloat16)
        flattened_rows = normed.reshape(CONTEXT_BLOCKS * BLOCK_TOKENS, MODEL_WIDTH)
        queries = rotary_embed(jnp.dot(flattened_rows, w_query[current_layer], preferred_element_type=jnp.float32).reshape(CONTEXT_BLOCKS, BLOCK_TOKENS, HQ, HEAD_SIZE), token_positions).astype(jnp.bfloat16)
        projected_keys = rotary_embed(jnp.dot(flattened_rows, key_weight[current_layer], preferred_element_type=jnp.float32).reshape(CONTEXT_BLOCKS, BLOCK_TOKENS, KEY_VALUE_HEADS, HEAD_SIZE), token_positions).astype(jnp.bfloat16)
        projected_values = jnp.dot(flattened_rows, value_weight[current_layer], preferred_element_type=jnp.float32).reshape(CONTEXT_BLOCKS, BLOCK_TOKENS, KEY_VALUE_HEADS, HEAD_SIZE).astype(jnp.bfloat16)
        attended = attend(queries, projected_keys, projected_values, block_ids, projected_keys[0], projected_values[0]).reshape(CONTEXT_BLOCKS * BLOCK_TOKENS, HQ * HEAD_SIZE)
        totals = jnp.zeros((CONTEXT_BLOCKS * BLOCK_TOKENS, MODEL_WIDTH), jnp.float32)
        for shard in range(N_TP):
            partial_sum = jnp.dot(attended[:, shard * share:(shard + 1) * share], w_out[current_layer][shard * share:(shard + 1) * share], preferred_element_type=jnp.float32).astype(jnp.bfloat16)
            totals = totals + lax.optimization_barrier(partial_sum).astype(jnp.float32)
        state = (values32 + totals.reshape(CONTEXT_BLOCKS, BLOCK_TOKENS, MODEL_WIDTH)).astype(jnp.bfloat16)
        layer_outputs.append(state)
    return jnp.stack(layer_outputs)
```

```python
import jax
import jax.numpy as jnp
from jax import lax
from jax.sharding import PartitionSpec as P

HEAD_SIZE = 128


rope_theta = 500000.0
norm_eps = 1e-05


def shift(block, axis, distance):
    size = lax.axis_size(axis)
    return lax.ppermute(block, axis, [(i, (i + distance) % size) for i in range(size)])


def from_behind(block, axis, distance):
    devices = range(lax.axis_size(axis))
    route = [(i - distance, i) for i in devices if i - distance in devices]
    return lax.ppermute(block, axis, route)


def broadcast_anchor(block):
    size = lax.axis_size("ctx")
    chips = size // 2
    me = lax.axis_index("ctx")
    pair = lax.ppermute(block, "ctx", [(0, 1)])
    root = jnp.where(me == 0, block, pair)
    up = [(0, 2 * z) for z in range(1, chips // 2 + 1)]
    down = [(1, 2 * z + 1) for z in range(chips - 1, chips // 2, -1)]
    parts = []
    for step in range(len(up)):
        route = [up[step]] + ([down[step]] if step < len(down) else [])
        parts.append(lax.ppermute(root, "ctx", route))
    total = jnp.where(me < 2, root, jnp.zeros_like(root))
    for part in parts:
        total = total + part
    twin = lax.ppermute(
        total, "ctx", [(d, d + 1) for _, d in up] + [(d, d - 1) for _, d in down]
    )
    return total + twin


def rotary_tables(token_positions, head_dim):
    half_size = head_dim // 2
    frequency = rope_theta ** (-(jnp.arange(half_size, dtype=jnp.float32) * 2.0 / head_dim))
    angles = token_positions[:, None] * frequency[None, :]
    cosine = jnp.concatenate([jnp.cos(angles), jnp.cos(angles)], -1)[:, None, :]
    sine_part = jnp.concatenate([-jnp.sin(angles), jnp.sin(angles)], -1)[:, None, :]
    return cosine, sine_part


def rotary_embed(values, tables):
    cosine, sine_part = tables
    half_size = values.shape[-1] // 2
    rotated = jnp.concatenate([values[..., half_size:], values[..., :half_size]], -1)
    return values * cosine + rotated * sine_part


def project(chunks, tables, gain_row, query_map, key_map, value_map):
    rows = jnp.concatenate(chunks, 0)
    values32 = rows.astype(jnp.float32)
    scale_rows = lax.rsqrt(jnp.mean(values32 * values32, -1, keepdims=True) + norm_eps)
    normed = (values32 * scale_rows * gain_row.astype(jnp.float32)).astype(jnp.bfloat16)

    def heads(table):
        return jnp.dot(normed, table, preferred_element_type=jnp.float32).reshape(
            rows.shape[0], -1, HEAD_SIZE
        )

    keys = rotary_embed(heads(key_map), tables).astype(jnp.bfloat16)
    values = heads(value_map).astype(jnp.bfloat16)
    queries = rotary_embed(heads(query_map), tables).astype(jnp.bfloat16)
    return queries, keys, values


def attend(queries, keys, values, order, is_anchor, anchor_key, anchor_value):
    length, head_count, head_dim = queries.shape
    kv_heads = keys.shape[1]
    groups = head_count // kv_heads
    all_keys = jnp.concatenate([anchor_key, keys], 0)
    all_values = jnp.concatenate([anchor_value, values], 0)
    grouped = queries.reshape(length, kv_heads, groups, head_dim)
    scores = jnp.einsum(
        "qkgd,skd->kgqs", grouped, all_keys, preferred_element_type=jnp.float32
    ) / jnp.sqrt(jnp.float32(head_dim))
    own_ok = order[None, :] <= order[:, None]
    anchor_ok = jnp.broadcast_to(jnp.logical_not(is_anchor), (length, length))
    allowed = jnp.concatenate([anchor_ok, own_ok], 1)
    scores = jnp.where(allowed[None, None], scores, jnp.float32(-1e30))
    highest = jnp.max(scores, -1, keepdims=True)
    powers = jnp.exp(scores - highest)
    weights = (powers / jnp.sum(powers, -1, keepdims=True)).astype(jnp.bfloat16)
    mixed = jnp.einsum("kgqs,skd->qkgd", weights, all_values, preferred_element_type=jnp.float32)
    return mixed.astype(jnp.bfloat16).reshape(length, head_count * head_dim)


def per_device(hidden, norm_gain, w_query, key_weight, value_weight, w_out):
    section = lax.axis_index("pipe")
    sections = lax.axis_size("pipe")
    shards = lax.axis_size("tp")
    me = lax.axis_index("tp")
    block = lax.axis_index("ctx")
    share = hidden.shape[1]
    length = share * shards
    order = jnp.concatenate(
        [lax.rem(me - j + shards, shards) * share + jnp.arange(share) for j in range(shards)]
    )
    tables = rotary_tables((block * length + order).astype(jnp.float32), HEAD_SIZE)
    current = hidden[0]
    result = jnp.zeros_like(current)
    for tick in range(sections):
        chunks = [current] + [shift(current, "tp", j) for j in range(1, shards)]
        queries, keys, values = project(
            chunks, tables, norm_gain[0], w_query[0], key_weight[0], value_weight[0]
        )
        anchor = broadcast_anchor(jnp.stack([keys, values]))
        attended = attend(queries, keys, values, order, block == 0, anchor[0], anchor[1])
        terms = jnp.dot(attended, w_out[0], preferred_element_type=jnp.float32).astype(jnp.bfloat16)
        terms = terms.reshape(shards, share, -1)
        total = terms[0].astype(jnp.float32)
        for j in range(1, shards):
            total = total + shift(terms[j], "tp", -j).astype(jnp.float32)
        updated = (current.astype(jnp.float32) + total).astype(jnp.bfloat16)
        result = jnp.where(section == tick, updated, result)
        if tick + 1 < sections:
            current = from_behind(updated, "pipe", 1)
    return result[None, None]


def solution(mesh):
    placed = (
        P("ctx", "tp", None),
        P("pipe", None),
        P("pipe", None, "tp"),
        P("pipe", None, "tp"),
        P("pipe", None, "tp"),
        P("pipe", "tp", None),
    )
    return jax.shard_map(
        per_device,
        mesh=mesh,
        in_specs=placed,
        out_specs=P("pipe", "ctx", "tp", None),
        check_vma=False,
    )
```

```python
import jax
import jax.numpy as jnp
from jax import lax
from jax.sharding import PartitionSpec as P

HEAD_SIZE = 128


rope_theta = 500000.0
norm_eps = 1e-05


def after(value, *earlier):
    return lax.optimization_barrier((value, earlier))[0]


def ring(size, distance):
    return [(i, (i + distance) % size) for i in range(size)]


def swap_cores(block):
    return lax.ppermute(block, "ctx", [(i, i ^ 1) for i in range(lax.axis_size("ctx"))])


def gather(rows):
    size = lax.axis_size("tp")
    return [rows] + [lax.ppermute(rows, "tp", ring(size, j)) for j in range(1, size)]


def scatter(terms):
    size = lax.axis_size("tp")
    return [terms[0]] + [lax.ppermute(terms[j], "tp", ring(size, -j)) for j in range(1, size)]


def broadcast_anchor(block):
    size = lax.axis_size("ctx")
    chips = size // 2
    me = lax.axis_index("ctx")
    up = [(0, 2 * z) for z in range(1, chips // 2 + 1)]
    down = [(1, 2 * z + 1) for z in range(chips - 1, chips // 2, -1)]
    parts = []
    for step in range(len(up)):
        route = [up[step]] + ([down[step]] if step < len(down) else [])
        parts.append(lax.ppermute(block, "ctx", route))
    total = jnp.where(me < 2, block, jnp.zeros_like(block))
    for part in parts:
        total = total + part
    twin = lax.ppermute(
        total, "ctx", [(d, d + 1) for _, d in up] + [(d, d - 1) for _, d in down]
    )
    return total + twin


def rotary_tables(token_positions, head_dim):
    half_size = head_dim // 2
    frequency = rope_theta ** (-(jnp.arange(half_size, dtype=jnp.float32) * 2.0 / head_dim))
    angles = token_positions[:, None] * frequency[None, :]
    cosine = jnp.concatenate([jnp.cos(angles), jnp.cos(angles)], -1)[:, None, :]
    sine_part = jnp.concatenate([-jnp.sin(angles), jnp.sin(angles)], -1)[:, None, :]
    return cosine, sine_part


def rotary_embed(values, tables):
    cosine, sine_part = tables
    half_size = values.shape[-1] // 2
    rotated = jnp.concatenate([values[..., half_size:], values[..., :half_size]], -1)
    return values * cosine + rotated * sine_part


def project(chunks, tables, gain_row, query_map, key_map, value_map):
    rows = jnp.concatenate(chunks, 0)
    values32 = rows.astype(jnp.float32)
    scale_rows = lax.rsqrt(jnp.mean(values32 * values32, -1, keepdims=True) + norm_eps)
    normed = (values32 * scale_rows * gain_row.astype(jnp.float32)).astype(jnp.bfloat16)

    def heads(table):
        return jnp.dot(normed, table, preferred_element_type=jnp.float32).reshape(
            rows.shape[0], -1, HEAD_SIZE
        )

    keys = rotary_embed(heads(key_map), tables).astype(jnp.bfloat16)
    values = heads(value_map).astype(jnp.bfloat16)
    queries = rotary_embed(heads(query_map), tables).astype(jnp.bfloat16)
    return queries, jnp.stack([keys, values])


def attend(queries, query_order, pair, order, anchor, masked):
    length, head_count, head_dim = queries.shape
    kv_heads = pair.shape[2]
    groups = head_count // kv_heads
    both = jnp.concatenate([anchor, pair], 1)
    grouped = queries.reshape(length, kv_heads, groups, head_dim)
    scores = jnp.einsum(
        "qkgd,skd->kgqs", grouped, both[0], preferred_element_type=jnp.float32
    ) / jnp.sqrt(jnp.float32(head_dim))
    own_ok = order[None, :] <= query_order[:, None]
    anchor_ok = jnp.broadcast_to(jnp.logical_not(masked), own_ok.shape)
    allowed = jnp.concatenate([anchor_ok, own_ok], 1)
    scores = jnp.where(allowed[None, None], scores, jnp.float32(-1e30))
    highest = jnp.max(scores, -1, keepdims=True)
    powers = jnp.exp(scores - highest)
    weights = (powers / jnp.sum(powers, -1, keepdims=True)).astype(jnp.bfloat16)
    mixed = jnp.einsum("kgqs,skd->qkgd", weights, both[1], preferred_element_type=jnp.float32)
    return mixed.astype(jnp.bfloat16).reshape(length, head_count * head_dim)


def out_terms(attended, table, shards):
    terms = jnp.dot(attended, table, preferred_element_type=jnp.float32).astype(jnp.bfloat16)
    return list(terms.reshape(shards, -1, terms.shape[-1]))


def update(rows, parts):
    total = parts[0].astype(jnp.float32)
    for part in parts[1:]:
        total = total + part.astype(jnp.float32)
    return (rows.astype(jnp.float32) + total).astype(jnp.bfloat16)


def per_device(hidden, norm_gain, w_query, key_weight, value_weight, w_out):
    section = lax.axis_index("pipe")
    sections = lax.axis_size("pipe")
    shards = lax.axis_size("tp")
    me = lax.axis_index("tp")
    chip, core = lax.axis_index("ctx") // 2, lax.axis_index("ctx") % 2
    share = hidden.shape[1]
    half = share // 2
    length = share * shards
    first = core == 0

    def order_of(side):
        return jnp.concatenate(
            [
                lax.rem(me - j + shards, shards) * share + side * half + jnp.arange(half)
                for j in range(shards)
            ]
        )

    order = order_of(core)
    pair_order = jnp.concatenate([order, order_of(1 - core)])
    tables = [
        rotary_tables(((2 * chip + odd) * length + order).astype(jnp.float32), HEAD_SIZE)
        for odd in range(2)
    ]
    maps = (w_query[0], key_weight[0], value_weight[0])
    gain = norm_gain[0]

    got = swap_cores(jnp.where(first, hidden[0, half:], hidden[0, :half]))
    even = jnp.where(first, hidden[0, :half], got)
    odd = jnp.where(first, got, hidden[0, half:])
    even_result, odd_result = jnp.zeros_like(even), jnp.zeros_like(odd)
    hop = [(i, i + 1) for i in range(sections - 1)]
    for layer in range(sections):
        even_chunks = gather(even)
        even_queries, even_mine = project(even_chunks, tables[0], gain, *maps)
        even_pair = jnp.concatenate([even_mine, swap_cores(even_mine)], 1)
        odd_chunks = gather(after(odd, *even_chunks))
        anchor = broadcast_anchor(even_pair)
        odd_queries, odd_mine = project(odd_chunks, tables[1], gain, *maps)
        odd_pair = jnp.concatenate([odd_mine, swap_cores(odd_mine)], 1)

        attended = attend(even_queries, order, even_pair, pair_order, anchor, chip == 0)
        even_parts = scatter(out_terms(attended, w_out[0], shards))
        attended = attend(odd_queries, order, odd_pair, pair_order, anchor, False)
        odd_parts = scatter(after(out_terms(attended, w_out[0], shards), *even_parts))
        even_new = update(even, even_parts)
        odd_new = update(odd, odd_parts)
        even_result = jnp.where(section == layer, even_new, even_result)
        odd_result = jnp.where(section == layer, odd_new, odd_result)
        if layer + 1 < sections:
            even = lax.ppermute(even_new, "pipe", hop)
            odd = lax.ppermute(odd_new, "pipe", hop)
    got = swap_cores(jnp.where(first, odd_result, even_result))
    result = jnp.where(
        first, jnp.concatenate([even_result, got], 0), jnp.concatenate([got, odd_result], 0)
    )
    return result[None, None]


def solution(mesh):
    placed = (
        P("ctx", "tp", None),
        P("pipe", None),
        P("pipe", None, "tp"),
        P("pipe", None, "tp"),
        P("pipe", None, "tp"),
        P("pipe", "tp", None),
    )
    return jax.shard_map(
        per_device,
        mesh=mesh,
        in_specs=placed,
        out_specs=P("pipe", "ctx", "tp", None),
        check_vma=False,
    )
```

```python
import functools

import jax
import jax.numpy as jnp
from jax import lax
from jax.experimental import pallas as pl
from jax.experimental.pallas import tpu as pltpu
from jax.sharding import PartitionSpec as P

HEAD_SIZE = 128


rope_theta = 500000.0
norm_eps = 1e-05

PAIRED = [(0, 1), (1, 0), (2, 3), (3, 2)]
TP_ORDER = (1, 3, 2)
LIVE = {1: (0, 1), 2: (2, 3), 3: (2, 3)}
VMEM_LIMIT = 48 * 1024 * 1024


def send_tp(value, distance, blocks, sections):
    size, count = lax.axis_size("tp"), lax.axis_size("pipe")
    route = [
        ((b * count + s) * size + i, (b * count + s) * size + (i + distance) % size)
        for b in blocks
        for s in sections
        for i in range(size)
    ]
    return lax.ppermute(value, ("ctx", "pipe", "tp"), route)


def after(value, *earlier):
    return lax.optimization_barrier((value, earlier))[0]


def swap_sections(block):
    return lax.ppermute(block, "pipe", PAIRED)


def gather(rows, blocks, sections):
    size = lax.axis_size("tp")
    parts = {j: send_tp(rows, j, blocks, sections) for j in TP_ORDER}
    return [rows] + [parts[j] for j in range(1, size)]


def scatter(terms, blocks, sections):
    return [terms[0]] + [send_tp(terms[j], -j, blocks, sections) for j in TP_ORDER]


def update(rows, parts):
    total = parts[0].astype(jnp.float32)
    for part in parts[1:]:
        total = total + part.astype(jnp.float32)
    return (rows.astype(jnp.float32) + total).astype(jnp.bfloat16)


def broadcast_anchor(block, live):
    size, sections = lax.axis_size("ctx"), lax.axis_size("pipe")
    me = lax.axis_index("ctx")
    distance = size // 2
    while distance:
        pairs = [(a, a + distance) for a in range(0, size, 2 * distance)]
        route = [(a * sections + s, b * sections + s) for a, b in pairs for s in live]
        got = lax.ppermute(block, ("ctx", "pipe"), route)
        block = jnp.where(me % (2 * distance) == distance, got, block)
        distance //= 2
    return block


def rotary_tables(token_positions):
    half_size = HEAD_SIZE // 2
    frequency = rope_theta ** (-(jnp.arange(half_size, dtype=jnp.float32) * 2.0 / HEAD_SIZE))
    angles = token_positions.astype(jnp.float32)[:, None] * frequency[None, :]
    cosine, sine = jnp.cos(angles), jnp.sin(angles)
    return jnp.concatenate([cosine, cosine], -1), jnp.concatenate([-sine, sine], -1)


def project_kernel(chunk_count, refs):
    chunks = refs[:chunk_count]
    gain, cosine, sine, query_map, key_map, value_map = refs[chunk_count : chunk_count + 6]
    queries, pair, normed, query_sum, pair_sum = refs[chunk_count + 6 :]
    step, steps = pl.program_id(0), pl.num_programs(0)
    share = chunks[0].shape[0]
    depth = query_map.shape[0]

    @pl.when(step == 0)
    def _():
        for i, chunk in enumerate(chunks):
            values = chunk[...].astype(jnp.float32)
            scale = lax.rsqrt(jnp.mean(values * values, -1, keepdims=True) + norm_eps)
            scaled = values * scale * gain[...].astype(jnp.float32)
            normed[i * share : (i + 1) * share, :] = scaled.astype(jnp.bfloat16)
        query_sum[...] = jnp.zeros_like(query_sum)
        pair_sum[...] = jnp.zeros_like(pair_sum)

    rows = normed[:, pl.ds(pl.multiple_of(step * depth, depth), depth)]
    query_sum[...] += jnp.dot(rows, query_map[...], preferred_element_type=jnp.float32)
    width = key_map.shape[1]
    pair_sum[:, :width] += jnp.dot(rows, key_map[...], preferred_element_type=jnp.float32)
    pair_sum[:, width:] += jnp.dot(rows, value_map[...], preferred_element_type=jnp.float32)

    @pl.when(step == steps - 1)
    def _():
        def turn(values):
            return values * cosine[...] + pltpu.roll(values, HEAD_SIZE // 2, 1) * sine[...]

        for start in range(0, query_sum.shape[1], HEAD_SIZE):
            columns = slice(start, start + HEAD_SIZE)
            queries[:, columns] = turn(query_sum[:, columns]).astype(jnp.bfloat16)
        for start in range(0, width, HEAD_SIZE):
            columns = slice(start, start + HEAD_SIZE)
            pair[:, columns] = turn(pair_sum[:, columns]).astype(jnp.bfloat16)
        pair[:, width:] = pair_sum[:, width:].astype(jnp.bfloat16)


def project(chunks, gain_row, tables, maps, packed, query_width, kv_width):
    share, model = chunks[0].shape
    rows = share * len(chunks)
    steps = 1
    depth = model // steps

    def whole(shape):
        return pl.BlockSpec(shape, lambda k: (0, 0))

    if packed:
        maps = (maps, maps, maps)
        places = (0, query_width // kv_width, query_width // kv_width + 1)
    else:
        places = (0, 0, 0)
    widths = (query_width, kv_width, kv_width)
    map_specs = [
        pl.BlockSpec((depth, width), functools.partial(lambda place, k: (k, place), place))
        for width, place in zip(widths, places)
    ]

    def body(*refs):
        project_kernel(len(chunks), refs)

    return pl.pallas_call(
        body,
        grid=(steps,),
        out_shape=[
            jax.ShapeDtypeStruct((rows, query_width), jnp.bfloat16),
            jax.ShapeDtypeStruct((rows, 2 * kv_width), jnp.bfloat16),
        ],
        in_specs=[whole((share, model))] * len(chunks)
        + [whole((1, model)), whole((rows, HEAD_SIZE)), whole((rows, HEAD_SIZE))]
        + map_specs,
        out_specs=[whole((rows, query_width)), whole((rows, 2 * kv_width))],
        scratch_shapes=[
            pltpu.VMEM((rows, model), jnp.bfloat16),
            pltpu.VMEM((rows, query_width), jnp.float32),
            pltpu.VMEM((rows, 2 * kv_width), jnp.float32),
        ],
        compiler_params=pltpu.CompilerParams(
            dimension_semantics=("arbitrary",), vmem_limit_bytes=VMEM_LIMIT
        ),
        cost_estimate=pl.CostEstimate(
            flops=2 * rows * model * (query_width + 2 * kv_width),
            bytes_accessed=2 * model * (query_width + 2 * kv_width + rows),
            transcendentals=0,
        ),
    )(*chunks, gain_row[None], *tables, *maps)


def attend_kernel(pair_count, table_count, refs):
    queries, query_place, key_place = refs[:3]
    pairs = refs[3 : 3 + pair_count]
    tables = refs[3 + pair_count : 3 + pair_count + table_count]
    terms, attended = refs[3 + pair_count + table_count : -1], refs[-1]
    kv_width = pairs[0].shape[1] // 2
    groups = queries.shape[1] // kv_width
    half = queries.shape[1] // 2

    @pl.when(pl.program_id(0) == 0)
    def _():
        allowed = key_place[...] <= query_place[...]
        for head in range(queries.shape[1] // HEAD_SIZE):
            start = head // groups * HEAD_SIZE
            columns = slice(head * HEAD_SIZE, (head + 1) * HEAD_SIZE)
            scores = jnp.concatenate(
                [
                    lax.dot_general(
                        queries[:, columns],
                        pair[:, start : start + HEAD_SIZE],
                        (((1,), (1,)), ((), ())),
                        preferred_element_type=jnp.float32,
                    )
                    for pair in pairs
                ],
                1,
            ) * (1.0 / HEAD_SIZE**0.5)
            scores = jnp.where(allowed, scores, jnp.float32(-1e30))
            powers = jnp.exp(scores - jnp.max(scores, -1, keepdims=True))
            weights = (powers / jnp.sum(powers, -1, keepdims=True)).astype(jnp.bfloat16)
            mixed, place = 0.0, 0
            for pair in pairs:
                length = pair.shape[0]
                mixed += jnp.dot(
                    weights[:, place : place + length],
                    pair[:, kv_width + start : kv_width + start + HEAD_SIZE],
                    preferred_element_type=jnp.float32,
                )
                place += length
            attended[:, columns] = mixed.astype(jnp.bfloat16)

    def store(total, columns):
        share = terms[0].shape[0]
        for i, term in enumerate(terms):
            term[:, columns] = total[i * share : (i + 1) * share].astype(jnp.bfloat16)

    if table_count == 1:
        total = jnp.dot(attended[...], tables[0][...], preferred_element_type=jnp.float32)
        return store(total, slice(None))
    span = tables[0].shape[1]
    for start in range(0, terms[0].shape[1], span):
        group = slice(start // span * half, (start // span + 1) * half)
        total = jnp.dot(
            attended[:, :half], tables[0][group, :], preferred_element_type=jnp.float32
        ) + jnp.dot(attended[:, half:], tables[1][group, :], preferred_element_type=jnp.float32)
        store(total, slice(start, start + span))


def attend(queries, query_place, key_place, pairs, tables, shards):
    rows, width = queries.shape
    keys = key_place.shape[1]
    packed = len(tables) == 2
    model = tables[0].shape[0] if packed else tables[0].shape[1]
    steps = 1

    def whole(array):
        if array.ndim == 3:
            return pl.BlockSpec((None,) + array.shape[1:], lambda n: (0, 0, 0))
        return pl.BlockSpec(array.shape, lambda n: (0, 0))

    def body(*refs):
        attend_kernel(len(pairs), len(tables), refs)

    operands = [queries, query_place, key_place, *pairs]
    if packed:
        upper, lower = tables[0].shape[1] // (width // 2) - 2, tables[0].shape[1] // (width // 2) - 1
        table_specs = [
            pl.BlockSpec((model, width // 2), lambda n: (0, upper)),
            pl.BlockSpec((model, width // 2), lambda n: (0, lower)),
        ]
    else:
        table_specs = [whole(tables[0])]
    return pl.pallas_call(
        body,
        grid=(steps,),
        out_shape=[jax.ShapeDtypeStruct((rows // shards, model), jnp.bfloat16)] * shards,
        in_specs=[whole(operand) for operand in operands]
        + table_specs,
        out_specs=[pl.BlockSpec((rows // shards, model), lambda n: (0, 0))] * shards,
        scratch_shapes=[pltpu.VMEM((rows, width), jnp.bfloat16)],
        compiler_params=pltpu.CompilerParams(
            dimension_semantics=("arbitrary",), vmem_limit_bytes=VMEM_LIMIT
        ),
        cost_estimate=pl.CostEstimate(
            flops=2 * rows * width * (model + 2 * keys),
            bytes_accessed=2 * width * model + 2 * rows * (model + width),
            transcendentals=rows * keys * width // HEAD_SIZE,
        ),
    )(*operands, *tables)


def per_device(hidden, norm_gain, w_query, key_weight, value_weight, w_out):
    section = lax.axis_index("pipe")
    sections = lax.axis_size("pipe")
    shards = lax.axis_size("tp")
    me = lax.axis_index("tp")
    block = lax.axis_index("ctx")
    leads = block == 0
    share = hidden.shape[1]
    half = share // 2
    length = share * shards
    query_width, kv_width = w_query.shape[2], key_weight.shape[2]

    maps = (w_query[0], key_weight[0], value_weight[0])
    own_out = w_out[0]
    size = lax.axis_size("ctx")

    rows = maps[0].shape[0] // size
    depth, span = own_out.shape[0] // 2, own_out.shape[1] // size
    out_piece = lax.dynamic_slice_in_dim(own_out, block * span, span, 1)
    piece = [lax.dynamic_slice_in_dim(m, block * rows, rows, 0) for m in maps]
    piece = jnp.concatenate(piece + [out_piece[:depth], out_piece[depth:]], 1)
    other = lax.all_gather(swap_sections(piece), "ctx", tiled=True)
    gain = norm_gain[0]
    other_gain = swap_sections(gain)

    owners = lax.rem(me - jnp.arange(shards) + shards, shards)[:, None] * share

    def order_of(side):
        return (owners + side * half + jnp.arange(half)).reshape(-1)

    first = ([0], [0])
    whole = hidden[0]
    order = (owners + jnp.arange(share)).reshape(-1)
    queries, pair = project(
        gather(whole, *first), gain, rotary_tables(block * length + order), maps, False, query_width, kv_width
    )
    anchor = broadcast_anchor(pair, [0])
    new = update(whole, scatter(attend(queries, order[:, None], order[None], [pair], [own_out], shards), *first))
    moved = lax.ppermute(new[half:], ("ctx", "pipe", "tp"), [(i, shards + i) for i in range(shards)])

    side = jnp.where((section == 0) | (section == 3), 0, 1)
    current = jnp.where(
        leads,
        jnp.where(section == 0, new[:half], moved),
        jnp.where(side == 0, whole[:half], whole[half:]),
    )
    query_order = order_of(side)
    anchor_order = jnp.full((length,), jnp.where(leads, length, -1))
    key_order = jnp.concatenate([anchor_order, query_order, order_of(1 - side)])
    anchors = [jnp.where(section == 1, lax.ppermute(anchor, "pipe", [(0, 1)]), anchor)]
    tables = rotary_tables(block * length + query_order)
    query_place, key_place = lax.optimization_barrier((query_order[:, None], key_order[None]))
    steps = []
    for step in range(1, sections + 1):
        use_own = section == jnp.where(leads, step, step - 1)
        live = (range(step == sections, size), range(sections))
        chunks = gather(current, *live)
        gain_row = jnp.where(use_own, gain, other_gain)
        queries, mine = lax.cond(
            use_own,
            lambda chunks, row: project(chunks, row, tables, maps, False, query_width, kv_width),
            lambda chunks, row: project(chunks, row, tables, other, True, query_width, kv_width),
            chunks,
            gain_row,
        )
        theirs = swap_sections(mine)
        terms = lax.cond(
            use_own,
            lambda *args: attend(args[0], query_place, key_place, args[1:], [own_out], shards),
            lambda *args: attend(args[0], query_place, key_place, args[1:], [other, other], shards),
            queries,
            *anchors,
            mine,
            theirs,
        )
        if step < sections:
            anchor = broadcast_anchor(mine, LIVE[step])
            anchors = [anchor, swap_sections(anchor)]
        updated = update(current, scatter(terms, *live))
        steps.append((use_own, updated, swap_sections(updated)))
        current = updated
        if step <= 2:
            movers = [0] if step == 1 else range(1, size)
            route = [(c * sections + a, c * sections + b) for c in movers for a, b in ((0, 3), (1, 2))]
            hopped = lax.ppermute(updated, ("ctx", "pipe"), route)
            current = jnp.where(leads == (step == 1), hopped, updated)
    low, high = new[:half], new[half:]
    for use_own, updated, handed in steps:
        low = jnp.where(use_own, jnp.where(side == 0, updated, handed), low)
        high = jnp.where(use_own, jnp.where(side == 0, handed, updated), high)
    return jnp.concatenate([low, high], 0)[None, None]


def solution(mesh):
    placed = (
        P("ctx", "tp", None),
        P("pipe", None),
        P("pipe", None, "tp"),
        P("pipe", None, "tp"),
        P("pipe", None, "tp"),
        P("pipe", "tp", None),
    )
    return jax.shard_map(
        per_device,
        mesh=mesh,
        in_specs=placed,
        out_specs=P("pipe", "ctx", "tp", None),
        check_vma=False,
    )
```

```python
import functools

import jax
import jax.numpy as jnp
from jax import lax
from jax.experimental import pallas as pl
from jax.experimental.pallas import tpu as pltpu
from jax.sharding import PartitionSpec as P

HEAD_SIZE = 128


rope_theta = 500000.0
norm_eps = 1e-05

PAIRED = [(0, 1), (1, 0), (2, 3), (3, 2)]
TP_ORDER = (1, 3, 2)
LIVE = {1: (0, 1), 2: (2, 3), 3: (2, 3)}
VMEM_LIMIT = 48 * 1024 * 1024


def send_tp(value, distance, blocks, sections):
    size, count = lax.axis_size("tp"), lax.axis_size("pipe")
    route = [
        ((b * count + s) * size + i, (b * count + s) * size + (i + distance) % size)
        for b in blocks
        for s in sections
        for i in range(size)
    ]
    return lax.ppermute(value, ("ctx", "pipe", "tp"), route)


def after(value, *earlier):
    return lax.optimization_barrier((value, earlier))[0]


def swap_sections(block):
    return lax.ppermute(block, "pipe", PAIRED)


def gather(rows, blocks, sections):
    size = lax.axis_size("tp")
    parts = {j: send_tp(rows, j, blocks, sections) for j in TP_ORDER}
    return [rows] + [parts[j] for j in range(1, size)]


def scatter(terms, blocks, sections):
    return [terms[0]] + [send_tp(terms[j], -j, blocks, sections) for j in TP_ORDER]


def update(rows, parts):
    total = parts[0].astype(jnp.float32)
    for part in parts[1:]:
        total = total + part.astype(jnp.float32)
    return (rows.astype(jnp.float32) + total).astype(jnp.bfloat16)


def broadcast_anchor(block, live):
    size, sections = lax.axis_size("ctx"), lax.axis_size("pipe")
    chips = size // 2
    me = lax.axis_index("ctx")

    def send(value, pairs):
        route = [(a * sections + s, b * sections + s) for a, b in pairs for s in live]
        return lax.ppermute(value, ("ctx", "pipe"), route)

    pair = send(block, [(0, 1)])
    root = jnp.where(me == 0, block, pair)
    up = [(0, 2 * z) for z in range(1, chips // 2 + 1)]
    down = [(1, 2 * z + 1) for z in range(chips - 1, chips // 2, -1)]
    parts = []
    for step in range(len(up)):
        parts.append(send(root, [up[step]] + ([down[step]] if step < len(down) else [])))
    total = jnp.where(me < 2, root, jnp.zeros_like(root))
    for part in parts:
        total = total + part
    twin = send(total, [(d, d + 1) for _, d in up] + [(d, d - 1) for _, d in down])
    return total + twin


def rotary_tables(token_positions):
    half_size = HEAD_SIZE // 2
    frequency = rope_theta ** (-(jnp.arange(half_size, dtype=jnp.float32) * 2.0 / HEAD_SIZE))
    angles = token_positions.astype(jnp.float32)[:, None] * frequency[None, :]
    cosine, sine = jnp.cos(angles), jnp.sin(angles)
    return jnp.concatenate([cosine, cosine], -1), jnp.concatenate([-sine, sine], -1)


def project_kernel(chunk_count, refs):
    chunks = refs[:chunk_count]
    gain, cosine, sine, query_map, key_map, value_map = refs[chunk_count : chunk_count + 6]
    queries, pair, normed, query_sum, pair_sum = refs[chunk_count + 6 :]
    step, steps = pl.program_id(0), pl.num_programs(0)
    share = chunks[0].shape[0]
    depth = query_map.shape[0]

    @pl.when(step == 0)
    def _():
        for i, chunk in enumerate(chunks):
            values = chunk[...].astype(jnp.float32)
            scale = lax.rsqrt(jnp.mean(values * values, -1, keepdims=True) + norm_eps)
            scaled = values * scale * gain[...].astype(jnp.float32)
            normed[i * share : (i + 1) * share, :] = scaled.astype(jnp.bfloat16)
        query_sum[...] = jnp.zeros_like(query_sum)
        pair_sum[...] = jnp.zeros_like(pair_sum)

    rows = normed[:, pl.ds(pl.multiple_of(step * depth, depth), depth)]
    query_sum[...] += jnp.dot(rows, query_map[...], preferred_element_type=jnp.float32)
    width = key_map.shape[1]
    pair_sum[:, :width] += jnp.dot(rows, key_map[...], preferred_element_type=jnp.float32)
    pair_sum[:, width:] += jnp.dot(rows, value_map[...], preferred_element_type=jnp.float32)

    @pl.when(step == steps - 1)
    def _():
        def turn(values):
            return values * cosine[...] + pltpu.roll(values, HEAD_SIZE // 2, 1) * sine[...]

        for start in range(0, query_sum.shape[1], HEAD_SIZE):
            columns = slice(start, start + HEAD_SIZE)
            queries[:, columns] = turn(query_sum[:, columns]).astype(jnp.bfloat16)
        for start in range(0, width, HEAD_SIZE):
            columns = slice(start, start + HEAD_SIZE)
            pair[:, columns] = turn(pair_sum[:, columns]).astype(jnp.bfloat16)
        pair[:, width:] = pair_sum[:, width:].astype(jnp.bfloat16)


def project(chunks, gain_row, tables, maps, packed, query_width, kv_width):
    share, model = chunks[0].shape
    rows = share * len(chunks)
    steps = 1
    depth = model // steps

    def whole(shape):
        return pl.BlockSpec(shape, lambda k: (0, 0))

    if packed:
        maps = (maps, maps, maps)
        places = (0, query_width // kv_width, query_width // kv_width + 1)
    else:
        places = (0, 0, 0)
    widths = (query_width, kv_width, kv_width)
    map_specs = [
        pl.BlockSpec((depth, width), functools.partial(lambda place, k: (k, place), place))
        for width, place in zip(widths, places)
    ]

    def body(*refs):
        project_kernel(len(chunks), refs)

    return pl.pallas_call(
        body,
        grid=(steps,),
        out_shape=[
            jax.ShapeDtypeStruct((rows, query_width), jnp.bfloat16),
            jax.ShapeDtypeStruct((rows, 2 * kv_width), jnp.bfloat16),
        ],
        in_specs=[whole((share, model))] * len(chunks)
        + [whole((1, model)), whole((rows, HEAD_SIZE)), whole((rows, HEAD_SIZE))]
        + map_specs,
        out_specs=[whole((rows, query_width)), whole((rows, 2 * kv_width))],
        scratch_shapes=[
            pltpu.VMEM((rows, model), jnp.bfloat16),
            pltpu.VMEM((rows, query_width), jnp.float32),
            pltpu.VMEM((rows, 2 * kv_width), jnp.float32),
        ],
        compiler_params=pltpu.CompilerParams(
            dimension_semantics=("arbitrary",), vmem_limit_bytes=VMEM_LIMIT
        ),
        cost_estimate=pl.CostEstimate(
            flops=2 * rows * model * (query_width + 2 * kv_width),
            bytes_accessed=2 * model * (query_width + 2 * kv_width + rows),
            transcendentals=0,
        ),
    )(*chunks, gain_row, *tables, *maps)


def attend_kernel(pair_count, table_count, refs):
    queries, query_place, key_place = refs[:3]
    pairs = refs[3 : 3 + pair_count]
    tables = refs[3 + pair_count : 3 + pair_count + table_count]
    terms, attended = refs[3 + pair_count + table_count : -1], refs[-1]
    kv_width = pairs[0].shape[1] // 2
    groups = queries.shape[1] // kv_width
    half = queries.shape[1] // 2

    @pl.when(pl.program_id(0) == 0)
    def _():
        allowed = key_place[...] <= query_place[...]
        for head in range(queries.shape[1] // HEAD_SIZE):
            start = head // groups * HEAD_SIZE
            columns = slice(head * HEAD_SIZE, (head + 1) * HEAD_SIZE)
            scores = jnp.concatenate(
                [
                    lax.dot_general(
                        queries[:, columns],
                        pair[:, start : start + HEAD_SIZE],
                        (((1,), (1,)), ((), ())),
                        preferred_element_type=jnp.float32,
                    )
                    for pair in pairs
                ],
                1,
            ) * (1.0 / HEAD_SIZE**0.5)
            scores = jnp.where(allowed, scores, jnp.float32(-1e30))
            powers = jnp.exp(scores - jnp.max(scores, -1, keepdims=True))
            weights = (powers / jnp.sum(powers, -1, keepdims=True)).astype(jnp.bfloat16)
            mixed, place = 0.0, 0
            for pair in pairs:
                length = pair.shape[0]
                mixed += jnp.dot(
                    weights[:, place : place + length],
                    pair[:, kv_width + start : kv_width + start + HEAD_SIZE],
                    preferred_element_type=jnp.float32,
                )
                place += length
            attended[:, columns] = mixed.astype(jnp.bfloat16)

    def store(total, columns):
        share = terms[0].shape[0]
        for i, term in enumerate(terms):
            term[:, columns] = total[i * share : (i + 1) * share].astype(jnp.bfloat16)

    if table_count == 1:
        total = jnp.dot(attended[...], tables[0][...], preferred_element_type=jnp.float32)
        return store(total, slice(None))
    span = tables[0].shape[1]
    for start in range(0, terms[0].shape[1], span):
        group = slice(start // span * half, (start // span + 1) * half)
        total = jnp.dot(
            attended[:, :half], tables[0][group, :], preferred_element_type=jnp.float32
        ) + jnp.dot(attended[:, half:], tables[1][group, :], preferred_element_type=jnp.float32)
        store(total, slice(start, start + span))


def attend(queries, query_place, key_place, pairs, tables, shards):
    rows, width = queries.shape
    keys = key_place.shape[1]
    packed = len(tables) == 2
    model = tables[0].shape[0] if packed else tables[0].shape[1]
    steps = 1

    def whole(array):
        if array.ndim == 3:
            return pl.BlockSpec((None,) + array.shape[1:], lambda n: (0, 0, 0))
        return pl.BlockSpec(array.shape, lambda n: (0, 0))

    def body(*refs):
        attend_kernel(len(pairs), len(tables), refs)

    operands = [queries, query_place, key_place, *pairs]
    if packed:
        upper, lower = tables[0].shape[1] // (width // 2) - 2, tables[0].shape[1] // (width // 2) - 1
        table_specs = [
            pl.BlockSpec((model, width // 2), lambda n: (0, upper)),
            pl.BlockSpec((model, width // 2), lambda n: (0, lower)),
        ]
    else:
        table_specs = [whole(tables[0])]
    return pl.pallas_call(
        body,
        grid=(steps,),
        out_shape=[jax.ShapeDtypeStruct((rows // shards, model), jnp.bfloat16)] * shards,
        in_specs=[whole(operand) for operand in operands]
        + table_specs,
        out_specs=[pl.BlockSpec((rows // shards, model), lambda n: (0, 0))] * shards,
        scratch_shapes=[pltpu.VMEM((rows, width), jnp.bfloat16)],
        compiler_params=pltpu.CompilerParams(
            dimension_semantics=("arbitrary",), vmem_limit_bytes=VMEM_LIMIT
        ),
        cost_estimate=pl.CostEstimate(
            flops=2 * rows * width * (model + 2 * keys),
            bytes_accessed=2 * width * model + 2 * rows * (model + width),
            transcendentals=rows * keys * width // HEAD_SIZE,
        ),
    )(*operands, *tables)


def per_device(hidden, norm_gain, w_query, key_weight, value_weight, w_out):
    section = lax.axis_index("pipe")
    sections = lax.axis_size("pipe")
    shards = lax.axis_size("tp")
    me = lax.axis_index("tp")
    block = lax.axis_index("ctx")
    leads = block == 0
    share = hidden.shape[1]
    half = share // 2
    length = share * shards
    query_width, kv_width = w_query.shape[2], key_weight.shape[2]

    maps = (w_query[0], key_weight[0], value_weight[0])
    own_out = w_out[0]
    size = lax.axis_size("ctx")

    rows = maps[0].shape[0] // size
    depth, span = own_out.shape[0] // 2, own_out.shape[1] // size
    out_piece = lax.dynamic_slice_in_dim(own_out, block * span, span, 1)
    piece = [lax.dynamic_slice_in_dim(m, block * rows, rows, 0) for m in maps]
    piece = jnp.concatenate(piece + [out_piece[:depth], out_piece[depth:]], 1)
    other = lax.all_gather(swap_sections(piece), "ctx", tiled=True)
    other_gain = swap_sections(norm_gain)

    owners = lax.rem(me - jnp.arange(shards) + shards, shards)[:, None] * share

    def order_of(side):
        return (owners + side * half + jnp.arange(half)).reshape(-1)

    first = ([0], [0])
    whole = hidden[0]
    order = (owners + jnp.arange(share)).reshape(-1)
    queries, pair = project(
        gather(whole, *first), norm_gain, rotary_tables(block * length + order), maps, False, query_width, kv_width
    )
    anchor = broadcast_anchor(pair, [0])
    new = update(whole, scatter(attend(queries, order[:, None], order[None], [pair], [own_out], shards), *first))
    moved = lax.ppermute(new[half:], ("ctx", "pipe", "tp"), [(i, shards + i) for i in range(shards)])

    side = jnp.where((section == 0) | (section == 3), 0, 1)
    current = jnp.where(
        leads,
        jnp.where(section == 0, new[:half], moved),
        jnp.where(side == 0, whole[:half], whole[half:]),
    )
    query_order = order_of(side)
    anchor_order = jnp.full((length,), jnp.where(leads, length, -1))
    key_order = jnp.concatenate([anchor_order, query_order, order_of(1 - side)])
    anchors = [jnp.where(section == 1, lax.ppermute(anchor, "pipe", [(0, 1)]), anchor)]
    tables = rotary_tables(block * length + query_order)
    query_place, key_place = lax.optimization_barrier((query_order[:, None], key_order[None]))
    steps = []
    for step in range(1, sections + 1):
        use_own = section == jnp.where(leads, step, step - 1)
        live = (range(step == sections, size), range(sections))
        chunks = gather(current, *live)
        gain_row = jnp.where(use_own, norm_gain, other_gain)
        queries, mine = lax.cond(
            use_own,
            lambda chunks, row: project(chunks, row, tables, maps, False, query_width, kv_width),
            lambda chunks, row: project(chunks, row, tables, other, True, query_width, kv_width),
            chunks,
            gain_row,
        )
        theirs = swap_sections(mine)
        terms = lax.cond(
            use_own,
            lambda *args: attend(args[0], query_place, key_place, args[1:], [own_out], shards),
            lambda *args: attend(args[0], query_place, key_place, args[1:], [other, other], shards),
            queries,
            *anchors,
            mine,
            theirs,
        )
        if step < sections:
            anchors = [broadcast_anchor(jnp.concatenate([mine, theirs], 0), LIVE[step])]
        updated = update(current, scatter(terms, *live))
        steps.append((use_own, updated, swap_sections(updated)))
        current = updated
        if step <= 2:
            movers = [0] if step == 1 else range(1, size)
            route = [(c * sections + a, c * sections + b) for c in movers for a, b in ((0, 3), (1, 2))]
            hopped = lax.ppermute(updated, ("ctx", "pipe"), route)
            current = jnp.where(leads == (step == 1), hopped, updated)
    low, high = new[:half], new[half:]
    for use_own, updated, handed in steps:
        low = jnp.where(use_own, jnp.where(side == 0, updated, handed), low)
        high = jnp.where(use_own, jnp.where(side == 0, handed, updated), high)
    return jnp.concatenate([low, high], 0)[None, None]


def solution(mesh):
    placed = (
        P("ctx", "tp", None),
        P("pipe", None),
        P("pipe", None, "tp"),
        P("pipe", None, "tp"),
        P("pipe", None, "tp"),
        P("pipe", "tp", None),
    )
    return jax.shard_map(
        per_device,
        mesh=mesh,
        in_specs=placed,
        out_specs=P("pipe", "ctx", "tp", None),
        check_vma=False,
    )
```
